32 devices in a mesh: dp: 4 (over y, x), expert: 8 (over z, core).
Axes of the slice: x: 2, y: 2, z: 4, core: 2. Of those that a mesh axis runs over, the one named last changes fastest.
Arguments:
- tokens: bfloat16 [4096, 2048], P(('dp', 'expert')), may hold values from -6 to 6
- expert_ids: int32 [4096, 2], P(('dp', 'expert')), may hold values from 0 to 7, as said below
- gate_values: float32 [4096, 2], P(('dp', 'expert')), may hold values from 0.05 to 0.5
- gate_up: bfloat16 [8, 2048, 1024], P('expert'), may hold values from -0.125 to 0.125
- down: bfloat16 [8, 512, 2048], P('expert'), may hold values from -0.25 to 0.25
- moment_first: bfloat16 [8, 512, 2048], P('expert'), may hold values from -6 to 6
- moment_second: bfloat16 [8, 512, 2048], P('expert'), may hold values from 1 to 100
- cotangent: bfloat16 [4096, 2048], P(('dp', 'expert')), may hold values from -6 to 6
Outputs:
- mixed: bfloat16 [4096, 2048], P(('dp', 'expert'))
- new_down: bfloat16 [8, 512, 2048], P('expert')
- new_first: bfloat16 [8, 512, 2048], P('expert')
- new_second: bfloat16 [8, 512, 2048], P('expert')
The draws below stay inside these ranges and needn't reach their ends.
Inputs may be any that keep to these rules, and one draw needn't show every extreme that they name: `expert_ids`: each token names 2 different experts. In each data group one expert is named exactly 64 times by the tokens of every device of the group; every other expert is named at most 28 times by one device's tokens, and the other experts' counts on one device differ by one at most.
All inputs are finite; a program needn't handle non-finite values.
Results may differ from the reference program's by a relative error of at most 0.0058.
Values may be sent and summed in bfloat16 or wider, within the bound.
A program may use at most 128 MiB of HBM per device.

```python
import math
import jax
import jax.numpy as jnp
from jax import lax

D = 2048
FF = 512
TOK_DEV = 128
EXPERTS = 8
TOP = 2
CAP = 64
TOKENS = 4096
N_DP = 4
N_EXPERT = 8


def draw_expert_ids(key, part):
    key = jax.random.fold_in(key, 5)
    group_key = jax.random.fold_in(key, 1)
    busiest = jax.random.randint(group_key, (N_DP,), 0, EXPERTS).astype(jnp.int32)
    row_index = jnp.arange(TOK_DEV, dtype=jnp.int32)[:, None]
    col_index = jnp.arange(TOP, dtype=jnp.int32)[None, :]
    busy_token = row_index < CAP
    stream = jnp.where(busy_token, row_index * (TOP - 1) + col_index - 1, CAP * (TOP - 1) + (row_index - CAP) * TOP + col_index)

    def one_block(device):
        block_key = jax.random.fold_in(key, device + 7)
        key_one, key_two, key_three, key_four = jax.random.split(block_key, 4)
        busy = busiest[device // N_EXPERT]
        others = (busy + 1 + jax.random.permutation(key_one, EXPERTS - 1).astype(jnp.int32)) % EXPERTS
        offset = jax.random.randint(key_two, (), 0, EXPERTS - 1).astype(jnp.int32)
        picked = others[(stream + offset) % (EXPERTS - 1)]
        chosen = jnp.where(busy_token & (col_index == 0), busy, picked)
        chosen = chosen[jax.random.permutation(key_three, TOK_DEV)]
        turn = jax.random.randint(key_four, (TOK_DEV, 1), 0, TOP).astype(jnp.int32)
        return jnp.take_along_axis(chosen, (col_index + turn) % TOP, axis=1)
    blocks = jax.vmap(one_block)(jnp.arange(N_DP * N_EXPERT, dtype=jnp.int32))
    return blocks.reshape(TOKENS, TOP).astype(jnp.int32)


def block_scale(own_key, dims, cuts, low, largest):
    def one(axis_at, blocks):
        draws = jax.random.uniform(jax.random.fold_in(jax.random.fold_in(own_key, 6), axis_at), (blocks,), jnp.float32, low / len(cuts), largest / len(cuts))
        return jnp.repeat(jnp.exp(draws), dims[axis_at] // blocks).reshape((-1,) + (1,) * (len(dims) - axis_at - 1))

    loudness = one(*cuts[0])
    for cut in cuts[1:]:
        loudness = loudness * one(*cut)
    return loudness


def gaussian(rng, dims, spread, limit, shards=(), kind=jnp.bfloat16):
    gain = block_scale(rng, dims, shards, -0.22, 0.18) if shards else 1.0
    drawn = jax.random.normal(rng, dims, jnp.float32) * spread * gain
    return jnp.minimum(jnp.maximum(drawn, -limit), limit).astype(kind)


def setup_inputs(seed: int = 0) -> dict:
    keys = jax.random.split(jax.random.key(seed), 9)
    tokens = gaussian(keys[0], (TOKENS, D), 1.0, 6.0, ((0, 32),))
    expert_ids = draw_expert_ids(jax.random.fold_in(keys[8], 71), 0)
    gate_values = jnp.clip(jnp.exp(math.log(0.5) - 2.3025851 * jax.random.uniform(keys[2], (TOKENS, TOP), jnp.float32) ** block_scale(keys[2], (TOKENS, TOP), ((0, 32),), -0.2, 0.2)), 0.05, 0.5)
    gate_up = gaussian(keys[3], (EXPERTS, D, 2 * FF), D ** -0.5, 0.125, ((0, 8),))
    down = gaussian(keys[4], (EXPERTS, FF, D), FF ** -0.5, 0.25, ((0, 8),))
    moment_first = gaussian(keys[5], (EXPERTS, FF, D), 1.0, 6.0, ((0, 8),))
    moment_second = jnp.clip(jnp.exp(math.log(100.0) - 4.6051702 * jax.random.uniform(keys[6], (EXPERTS, FF, D), jnp.float32) ** block_scale(keys[6], (EXPERTS, FF, D), ((0, 8),), -0.2, 0.2)), 1.0, 100.0).astype(jnp.bfloat16)
    cotangent = gaussian(keys[7], (TOKENS, D), 1.0, 6.0, ((0, 32),))
    return {"tokens": tokens, "expert_ids": expert_ids, "gate_values": gate_values, "gate_up": gate_up, "down": down, "moment_first": moment_first, "moment_second": moment_second, "cotangent": cotangent}


beta_one = 0.9
beta_two = 0.95
learn_rate = 0.01
decay_rate = 0.1
eps_value = 1e-08
first_fix = 1.0 - 0.9 ** 10
second_fix = 1.0 - 0.95 ** 10

def expert_apply(rows, gate_up_w, down_w, feature_half):
    projected = jnp.dot(rows, gate_up_w, preferred_element_type=jnp.float32)
    hidden_act = (jax.nn.silu(projected[:, :feature_half]) * projected[:, feature_half:]).astype(jnp.bfloat16)
    expert_out = jnp.dot(hidden_act, down_w, preferred_element_type=jnp.float32).astype(jnp.bfloat16)
    return (hidden_act, expert_out)

def adamw(gradient, down_w, first_old, second_old):
    first_new = beta_one * first_old.astype(jnp.float32) + (1.0 - beta_one) * gradient
    second_new = beta_two * second_old.astype(jnp.float32) + (1.0 - beta_two) * gradient * gradient
    step_size = first_new / first_fix / (jnp.sqrt(second_new / second_fix) + eps_value)
    down_new = down_w.astype(jnp.float32) * (1.0 - learn_rate * decay_rate) - learn_rate * step_size
    return (down_new.astype(jnp.bfloat16), first_new.astype(jnp.bfloat16), second_new.astype(jnp.bfloat16))

def reference(tokens, expert_ids, gate_values, gate_up, down, moment_first, moment_second, cotangent):
    flat_ids = expert_ids.reshape(-1).astype(jnp.int32)
    assigns = flat_ids.shape[0]
    gate_flat = gate_values.reshape(-1)
    block_rows = CAP * N_EXPERT
    bound_rows = block_rows * N_DP
    positions = jnp.arange(assigns, dtype=jnp.int32)

    def per_expert(mixed_acc, expert_index):
        chosen = flat_ids == expert_index
        slot_rank = (jnp.cumsum(chosen.astype(jnp.int32)) - 1).astype(jnp.int32)
        chosen_count = jnp.sum(chosen.astype(jnp.int32))
        target = jnp.where(chosen, slot_rank, bound_rows).astype(jnp.int32)
        slot_source = jnp.full((bound_rows,), assigns, jnp.int32).at[target].set(positions, mode='drop')
        gate_w = gate_up[expert_index]
        down_w = down[expert_index]

        def compute(state, block_index):
            mixed_in, grad_in = state
            picked = lax.dynamic_slice_in_dim(slot_source, (block_index * block_rows).astype(jnp.int32), block_rows)
            filled = picked < assigns
            safe = jnp.minimum(picked, assigns - 1)
            token_of = (safe // TOP).astype(jnp.int32)
            rows = jnp.where(filled[:, None], tokens[token_of], jnp.zeros((), jnp.bfloat16))
            weight = jnp.where(filled, gate_flat[safe], jnp.zeros((), jnp.float32))
            hidden_act, expert_out = expert_apply(rows, gate_w, down_w, FF)
            scaled_rows = (weight[:, None] * cotangent[token_of].astype(jnp.float32)).astype(jnp.bfloat16)
            grad_in = grad_in + lax.dot_general(hidden_act, scaled_rows, (((0,), (0,)), ((), ())), preferred_element_type=jnp.float32)
            target_token = jnp.where(filled, token_of, TOKENS).astype(jnp.int32)
            mixed_in = mixed_in.at[target_token].add(weight[:, None] * expert_out.astype(jnp.float32), mode='drop')
            return (mixed_in, grad_in)

        def per_block(state, block_index):

            def run_block(inner):
                return compute(inner, block_index)

            def keep_block(inner):
                return inner
            result = lax.cond(block_index * block_rows < chosen_count, run_block, keep_block, state)
            return (result, None)
        start = (mixed_acc, jnp.zeros((FF, D), jnp.float32))
        (mixed_acc, gradient), unused = lax.scan(per_block, start, jnp.arange(N_DP, dtype=jnp.int32))
        return (mixed_acc, gradient)
    mixed_total, gradients = lax.scan(per_expert, jnp.zeros((TOKENS, D), jnp.float32), jnp.arange(EXPERTS, dtype=jnp.int32))
    new_down, new_first, new_second = adamw(gradients, down, moment_first, moment_second)
    return (mixed_total.astype(jnp.bfloat16), new_down, new_first, new_second)
```

```python
import jax
import jax.numpy as jnp
from jax import lax
from jax.experimental import pallas as pl
from jax.experimental.pallas import tpu as pltpu
from jax.sharding import PartitionSpec as P

beta_one = 0.9
beta_two = 0.95
learn_rate = 0.01
decay_rate = 0.1
eps_value = 1e-08
first_fix = 1.0 - 0.9**10
second_fix = 1.0 - 0.95**10


def expert_apply(rows, gate_up_w, down_w, feature_half):
    projected = jnp.dot(rows, gate_up_w, preferred_element_type=jnp.float32)
    hidden_act = (jax.nn.silu(projected[:, :feature_half]) * projected[:, feature_half:]).astype(
        jnp.bfloat16
    )
    expert_out = jnp.dot(hidden_act, down_w, preferred_element_type=jnp.float32).astype(
        jnp.bfloat16
    )
    return (hidden_act, expert_out)


def adamw(gradient, down_w, first_old, second_old):
    first_new = beta_one * first_old.astype(jnp.float32) + (1.0 - beta_one) * gradient
    second_new = beta_two * second_old.astype(jnp.float32) + (1.0 - beta_two) * gradient * gradient
    step_size = first_new / first_fix / (jnp.sqrt(second_new / second_fix) + eps_value)
    down_new = down_w.astype(jnp.float32) * (1.0 - learn_rate * decay_rate) - learn_rate * step_size
    return (
        down_new.astype(jnp.bfloat16),
        first_new.astype(jnp.bfloat16),
        second_new.astype(jnp.bfloat16),
    )


def outer_sum(hidden_act, scaled_rows):
    return lax.dot_general(
        hidden_act, scaled_rows, (((0,), (0,)), ((), ())), preferred_element_type=jnp.float32
    )


def body(tokens, expert_ids, gate_values, gate_up, down, moment_first, moment_second, cotangent):
    tok_rows, feature_count = tokens.shape
    top_count = expert_ids.shape[1]
    hidden_count = down.shape[1]
    experts = lax.axis_size("expert")
    capacity = tok_rows // 2
    flat_ids = expert_ids.reshape(-1)
    assigns = flat_ids.shape[0]
    positions = jnp.arange(assigns, dtype=jnp.int32)
    onehot = (flat_ids[:, None] == jnp.arange(experts, dtype=jnp.int32)[None, :]).astype(jnp.int32)
    slot_rank = jnp.sum((jnp.cumsum(onehot, axis=0) - 1) * onehot, axis=1)
    scaled = (
        (gate_values[:, :, None] * cotangent[:, None, :].astype(jnp.float32))
        .astype(jnp.bfloat16)
        .reshape(assigns, feature_count)
    )
    zero_value = jnp.zeros((), jnp.bfloat16)
    send_mask = flat_ids >= 0
    bucket_rows = experts * capacity
    slot_index = flat_ids * capacity + slot_rank
    target = jnp.where(send_mask, slot_index, bucket_rows)
    slot_source = (
        jnp.full((bucket_rows,), assigns, jnp.int32).at[target].set(positions, mode="drop")
    )
    filled = slot_source < assigns
    safe = jnp.minimum(slot_source, assigns - 1)
    sent_rows = jnp.where(filled[:, None], tokens[safe // top_count], zero_value).reshape(
        experts, capacity, feature_count
    )
    sent_scaled = jnp.where(filled[:, None], scaled[safe], zero_value).reshape(
        experts, capacity, feature_count
    )
    recv_rows, recv_scaled = (
        lax.all_to_all(sent_rows, "expert", split_axis=0, concat_axis=0, tiled=True),
        lax.all_to_all(sent_scaled, "expert", split_axis=0, concat_axis=0, tiled=True),
    )
    hidden_act, expert_out = expert_apply(
        recv_rows.reshape(bucket_rows, feature_count), gate_up[0], down[0], hidden_count
    )
    gradient = outer_sum(hidden_act, recv_scaled.reshape(bucket_rows, feature_count))
    returned_rows = lax.all_to_all(
        expert_out.reshape(experts, capacity, feature_count),
        "expert",
        split_axis=0,
        concat_axis=0,
        tiled=True,
    )
    returned_rows = returned_rows.reshape(bucket_rows, feature_count)
    picked = returned_rows[jnp.where(send_mask, slot_index, 0)]
    weighted = gate_values[:, :, None] * picked.reshape(tok_rows, top_count, feature_count).astype(
        jnp.float32
    )
    mixed = jnp.sum(weighted, axis=1).astype(jnp.bfloat16)
    gradient = lax.psum(gradient, "dp")
    new_down, new_first, new_second = adamw(gradient, down[0], moment_first[0], moment_second[0])
    return (mixed, new_down[None], new_first[None], new_second[None])


MESH = pl.DeviceIdType.MESH
CHUNKS = 4
SIDE = 4
EXPERTS = 8


def fused_kernel(
    weights_ref, tokens_ref, cot_ref, gate_up_hbm, down_hbm, first_hbm, second_hbm,
    mixed_ref, new_down_ref, new_first_ref, new_second_ref,
    gate_up, down, first_old, second_old,
    toks, cots, w_recv, w_cols, hidden, hidden_t, scaled, parts, peer_parts, from_left,
    from_right, acc, grad, grad_send, grad_recv, grad_all, acc_grad,
    load_sem, w_send, w_recv_sem, tok_send, tok_recv, cot_send, cot_recv,
    part_send, part_recv, sum_send, left_recv, right_recv, gs_send, gs_recv, ga_send, ga_recv,
):
    expert = lax.axis_index("expert")
    group = lax.axis_index("dp")
    chip = expert // 2
    core = expert % 2
    other = 1 - core
    rows, width = tokens_ref.shape
    half = down.shape[0]
    cw = width // CHUNKS
    quarter = half // 4
    group_x, group_y = group % 2, group // 2
    peer = chip * 2 + other
    right = jnp.minimum(chip + 1, SIDE - 1) * 2 + core
    left = jnp.maximum(chip - 1, 0) * 2 + core

    def dp_peer(k):
        px = group_x if k == 2 else 1 - group_x
        py = group_y if k == 1 else 1 - group_y
        return py * 2 + px

    def order(j):
        near = chip + 1 - 2 * (chip % 2)
        low = chip < 2
        return (chip, near, jnp.where(low, 2, 1), jnp.where(low, 3, 0))[j]

    def remote(src, dst, send, recv, target, axis="expert"):
        return pltpu.make_async_remote_copy(
            src_ref=src, dst_ref=dst, send_sem=send, recv_sem=recv,
            device_id={axis: target}, device_id_type=MESH,
        )

    loads = [
        pltpu.make_async_copy(src, dst, load_sem.at[i])
        for i, (src, dst) in enumerate(
            (
                (gate_up_hbm.at[0], gate_up),
                (down_hbm.at[0], down),
                (first_hbm.at[0], first_old),
                (second_hbm.at[0], second_old),
            )
        )
    ]
    for load in loads:
        load.start()

    barrier = pltpu.get_barrier_semaphore()
    for k in range(1, EXPERTS):
        pl.semaphore_signal(
            barrier, inc=1, device_id={"expert": (expert + k) % EXPERTS}, device_id_type=MESH
        )
    for k in range(1, 4):
        pl.semaphore_signal(barrier, inc=1, device_id={"dp": dp_peer(k)}, device_id_type=MESH)
    toks[chip, core] = tokens_ref[...]
    for n in range(CHUNKS):
        cots[n, chip, core] = cot_ref[:, n * cw : (n + 1) * cw]
    w_recv[expert] = weights_ref[expert]
    pl.semaphore_wait(barrier, EXPERTS + 2)

    def w_copy(k):
        target = (expert + k) % EXPERTS
        return remote(
            weights_ref.at[target], w_recv.at[expert], w_send.at[k - 1], w_recv_sem.at[k - 1], target
        )

    def w_arrival(k):
        source = (expert + EXPERTS - k) % EXPERTS
        return remote(
            weights_ref.at[source], w_recv.at[source], w_send.at[k - 1], w_recv_sem.at[k - 1], source
        )

    def gather_copies(buf, send, recv, j):
        b = order(j)
        block = buf.at[b, core]
        return (
            remote(block, block, send.at[j, 0], recv.at[b, core], right),
            remote(block, block, send.at[j, 1], recv.at[b, core], left),
            remote(block, block, send.at[j, 2], recv.at[b, core], peer),
        )

    def forward(buf, send, recv, j):
        b = order(j)
        to_right, to_left, to_peer = gather_copies(buf, send, recv, j)
        if j > 0:
            to_right.wait_recv()

        @pl.when((b <= chip) & (chip < SIDE - 1))
        def _():
            to_right.start()

        @pl.when((b >= chip) & (chip > 0))
        def _():
            to_left.start()

        to_peer.start()

    def from_peer(buf, send, recv, j):
        b = order(j)
        block = buf.at[b, other]
        remote(block, block, send.at[j, 2], recv.at[b, other], peer).wait_recv()

    def drain(buf, send, recv, j):
        b = order(j)
        to_right, to_left, to_peer = gather_copies(buf, send, recv, j)

        @pl.when((b <= chip) & (chip < SIDE - 1))
        def _():
            to_right.wait_send()

        @pl.when((b >= chip) & (chip > 0))
        def _():
            to_left.wait_send()

        to_peer.wait_send()

    tok_args = (toks, tok_send, tok_recv)

    def cot_args(n):
        return (cots.at[n], cot_send.at[n], cot_recv.at[n])

    def part_copy(b):
        return remote(
            parts.at[b, other], peer_parts.at[b], part_send.at[b], part_recv.at[b], peer
        )

    def run_expert(j):
        b = order(j)
        tile = 256

        @pl.loop(0, half // tile)
        def _(n):
            x = toks[b].reshape(2 * rows, width)
            lo = pl.multiple_of(n * tile, tile)
            hi = pl.multiple_of(half + n * tile, tile)
            gate = jnp.dot(x, gate_up[:, pl.ds(lo, tile)], preferred_element_type=jnp.float32)
            up = jnp.dot(x, gate_up[:, pl.ds(hi, tile)], preferred_element_type=jnp.float32)
            act = gate / (1.0 + jnp.exp(-gate)) * up
            hidden[:, pl.ds(lo, tile)] = act.astype(jnp.bfloat16)
            at = pl.multiple_of(b * 2 * rows, 2 * rows)
            hidden_t[pl.ds(lo, tile), pl.ds(at, 2 * rows)] = act.T.astype(jnp.bfloat16)

        @pl.loop(0, width // 512)
        def _(n):
            at = pl.multiple_of(n * 512, 512)
            out = jnp.dot(
                hidden[...], down[:, pl.ds(at, 512)], preferred_element_type=jnp.float32
            )
            w = w_cols[b].reshape(2 * rows, 128)[:, 0:1]
            parts[b, :, :, pl.ds(at, 512)] = (w * out).astype(jnp.bfloat16).reshape(2, rows, 512)

        part_copy(b).start()

    def sum_copies(b):
        block = parts.at[b, core]
        return (
            remote(block, from_left.at[b], sum_send.at[b], left_recv.at[b], right),
            remote(block, from_right.at[b], sum_send.at[b], right_recv.at[b], left),
        )

    def reduce_step(j):
        b = order(j)
        to_right, to_left = sum_copies(b)
        part_copy(b).wait_recv()
        acc[...] = parts[b, core].astype(jnp.float32) + peer_parts[b].astype(jnp.float32)

        @pl.when((b >= chip) & (chip > 0))
        def _():
            to_right.wait_recv()
            acc[...] += from_left[b].astype(jnp.float32)

        @pl.when((b <= chip) & (chip < SIDE - 1))
        def _():
            to_left.wait_recv()
            acc[...] += from_right[b].astype(jnp.float32)

        if j == 0:
            mixed_ref[...] = acc[...].astype(jnp.bfloat16)
        else:
            parts[b, core] = acc[...].astype(jnp.bfloat16)

            @pl.when(b > chip)
            def _():
                to_right.start()

            @pl.when(b < chip)
            def _():
                to_left.start()

    def scatter_copy(n, k):
        return remote(
            grad_send.at[n, dp_peer(k)], grad_recv.at[n, k - 1], gs_send.at[n, k - 1],
            gs_recv.at[n, k - 1], dp_peer(k), "dp",
        )

    def spread_copy(n, k, owner):
        block = grad_all.at[n, owner]
        return remote(
            block, block, ga_send.at[n, k - 1], ga_recv.at[n, k - 1], dp_peer(k), "dp"
        )

    def gradient(n):
        @pl.loop(0, SIDE)
        def _(b):
            w = w_cols[b].reshape(2 * rows, 128)[:, 0:1]
            cot = cots[n, b].reshape(2 * rows, cw).astype(jnp.float32)
            scaled[pl.ds(pl.multiple_of(b * 2 * rows, 2 * rows), 2 * rows), :] = (w * cot).astype(
                jnp.bfloat16
            )

        @pl.loop(0, 2)
        def _(m):
            at = pl.multiple_of(m * 2 * quarter, 2 * quarter)
            g = jnp.dot(
                hidden_t[pl.ds(at, 2 * quarter), :], scaled[...], preferred_element_type=jnp.float32
            )
            g = g.reshape(2, quarter, cw)
            grad[pl.ds(m * 2, 2)] = g
            grad_send[n, pl.ds(m * 2, 2)] = g.astype(jnp.bfloat16)

        for k in range(1, 4):
            scatter_copy(n, k).start()
        acc_grad[n] = grad[group]

    def spread(n):
        total = acc_grad[n]
        for k in range(1, 4):
            scatter_copy(n, k).wait_recv()
            total = total + grad_recv[n, k - 1].astype(jnp.float32)
        grad_all[n, group] = total.astype(jnp.bfloat16)
        for k in range(1, 4):
            spread_copy(n, k, group).start()

    def update(n):
        for k in range(1, 4):
            spread_copy(n, k, dp_peer(k)).wait_recv()
        columns = pl.ds(n * cw, cw)

        @pl.loop(0, half // 32)
        def _(i):
            at = pl.ds(pl.multiple_of(i * 32, 32), 32)
            per = quarter // 32
            g = grad_all[n, i // per, pl.ds(pl.multiple_of((i % per) * 32, 32), 32), :]
            new_down, new_first, new_second = adamw(
                g.astype(jnp.float32), down[at, columns], first_old[at, columns],
                second_old[at, columns],
            )
            new_down_ref[0, at, columns] = new_down
            new_first_ref[0, at, columns] = new_first
            new_second_ref[0, at, columns] = new_second

    for k in range(1, EXPERTS):
        w_copy(k).start()
    forward(*tok_args, 0)
    for k in range(1, EXPERTS):
        w_arrival(k).wait_recv()
    for s in range(EXPERTS):
        w_cols[s // 2, s % 2] = jnp.broadcast_to(w_recv[s][0:1, :], (128, 128)).T
    loads[0].wait()
    loads[1].wait()
    for j in range(SIDE):
        if j > 0:
            forward(*tok_args, j)
        if j == 2:
            forward(*cot_args(0), 0)
        from_peer(*tok_args, j)
        run_expert(j)
    loads[2].wait()
    loads[3].wait()
    for n in range(CHUNKS):
        forward(*cot_args(n), 1)
        if n + 1 < CHUNKS:
            forward(*cot_args(n + 1), 0)
        forward(*cot_args(n), 2)
        reduce_step(SIDE - 1 - n)
        forward(*cot_args(n), 3)
        for j in range(SIDE):
            from_peer(*cot_args(n), j)
        gradient(n)
        if n >= 1:
            spread(n - 1)
        if n >= 2:
            update(n - 2)
    spread(CHUNKS - 1)
    update(CHUNKS - 2)
    update(CHUNKS - 1)
    for j in range(SIDE):
        drain(*tok_args, j)
        for n in range(CHUNKS):
            drain(*cot_args(n), j)
        part_copy(order(j)).wait_send()
        if j > 0:
            sum_copies(order(j))[0].wait_send()
    for k in range(1, EXPERTS):
        w_copy(k).wait_send()
    for n in range(CHUNKS):
        for k in range(1, 4):
            scatter_copy(n, k).wait_send()
            spread_copy(n, k, group).wait_send()


def fused_body(tokens, expert_ids, gate_values, gate_up, down, first, second, cotangent):
    rows, width = tokens.shape
    half = down.shape[1]
    cw = width // CHUNKS
    quarter = half // 4
    chosen = expert_ids[None] == jnp.arange(EXPERTS, dtype=jnp.int32)[:, None, None]
    weights = jnp.sum(jnp.where(chosen, gate_values[None], 0.0), axis=2)
    weights = jnp.broadcast_to(weights[:, None, :], (EXPERTS, 8, rows))
    bf, f32 = jnp.bfloat16, jnp.float32
    vmem = pl.BlockSpec(memory_space=pltpu.VMEM)
    hbm = pl.BlockSpec(memory_space=pl.ANY)
    dma = pltpu.SemaphoreType.DMA
    buffers = [
        ((width, 2 * half), bf), ((half, width), bf), ((half, width), bf), ((half, width), bf),
        ((SIDE, 2, rows, width), bf), ((CHUNKS, SIDE, 2, rows, cw), bf),
        ((EXPERTS, 8, rows), f32), ((SIDE, 2, rows, 128), f32),
        ((2 * rows, half), bf), ((half, EXPERTS * rows), bf), ((EXPERTS * rows, cw), bf),
        ((SIDE, 2, rows, width), bf), ((SIDE, rows, width), bf), ((SIDE, rows, width), bf),
        ((SIDE, rows, width), bf), ((rows, width), f32), ((4, quarter, cw), f32),
        ((CHUNKS, 4, quarter, cw), bf), ((CHUNKS, 3, quarter, cw), bf),
        ((CHUNKS, 4, quarter, cw), bf), ((CHUNKS, quarter, cw), f32),
    ]
    semaphores = [
        (4,), (EXPERTS - 1,), (EXPERTS - 1,), (SIDE, 3), (SIDE, 2), (CHUNKS, SIDE, 3),
        (CHUNKS, SIDE, 2), (SIDE,), (SIDE,), (SIDE,), (SIDE,), (SIDE,), (CHUNKS, 3), (CHUNKS, 3),
        (CHUNKS, 3), (CHUNKS, 3),
    ]
    state = jax.ShapeDtypeStruct((1, half, width), bf)
    return pl.pallas_call(
        fused_kernel,
        out_shape=(jax.ShapeDtypeStruct((rows, width), bf), state, state, state),
        in_specs=[vmem, vmem, vmem, hbm, hbm, hbm, hbm],
        out_specs=(vmem, vmem, vmem, vmem),
        scratch_shapes=[pltpu.VMEM(s, t) for s, t in buffers] + [dma(s) for s in semaphores],
        compiler_params=pltpu.CompilerParams(
            collective_id=0, has_side_effects=True, vmem_limit_bytes=60 * 1024 * 1024
        ),
    )(weights, tokens, cotangent, gate_up, down, first, second)


def solution(mesh):
    def choose(*args):
        fits = mesh.shape["expert"] == 8 and mesh.shape["dp"] == 4 and args[0].shape[0] == 128
        return (fused_body if fits else body)(*args)

    return jax.shard_map(
        choose,
        mesh=mesh,
        in_specs=(
            P(("dp", "expert"), None),
            P(("dp", "expert"), None),
            P(("dp", "expert"), None),
            P("expert", None, None),
            P("expert", None, None),
            P("expert", None, None),
            P("expert", None, None),
            P(("dp", "expert"), None),
        ),
        out_specs=(
            P(("dp", "expert"), None),
            P("expert", None, None),
            P("expert", None, None),
            P("expert", None, None),
        ),
        check_vma=False,
    )
```

```python
import jax
import jax.numpy as jnp
from jax import lax
from jax.experimental import pallas as pl
from jax.experimental.pallas import tpu as pltpu
from jax.sharding import PartitionSpec as P

beta_one = 0.9
beta_two = 0.95
learn_rate = 0.01
decay_rate = 0.1
eps_value = 1e-08
first_fix = 1.0 - 0.9**10
second_fix = 1.0 - 0.95**10


def expert_apply(rows, gate_up_w, down_w, feature_half):
    projected = jnp.dot(rows, gate_up_w, preferred_element_type=jnp.float32)
    hidden_act = (jax.nn.silu(projected[:, :feature_half]) * projected[:, feature_half:]).astype(
        jnp.bfloat16
    )
    expert_out = jnp.dot(hidden_act, down_w, preferred_element_type=jnp.float32).astype(
        jnp.bfloat16
    )
    return (hidden_act, expert_out)


def adamw(gradient, down_w, first_old, second_old):
    first_new = beta_one * first_old.astype(jnp.float32) + (1.0 - beta_one) * gradient
    second_new = beta_two * second_old.astype(jnp.float32) + (1.0 - beta_two) * gradient * gradient
    step_size = first_new / first_fix / (jnp.sqrt(second_new / second_fix) + eps_value)
    down_new = down_w.astype(jnp.float32) * (1.0 - learn_rate * decay_rate) - learn_rate * step_size
    return (
        down_new.astype(jnp.bfloat16),
        first_new.astype(jnp.bfloat16),
        second_new.astype(jnp.bfloat16),
    )


def outer_sum(hidden_act, scaled_rows):
    return lax.dot_general(
        hidden_act, scaled_rows, (((0,), (0,)), ((), ())), preferred_element_type=jnp.float32
    )


def body(tokens, expert_ids, gate_values, gate_up, down, moment_first, moment_second, cotangent):
    tok_rows, feature_count = tokens.shape
    top_count = expert_ids.shape[1]
    hidden_count = down.shape[1]
    experts = lax.axis_size("expert")
    capacity = tok_rows // 2
    flat_ids = expert_ids.reshape(-1)
    assigns = flat_ids.shape[0]
    positions = jnp.arange(assigns, dtype=jnp.int32)
    onehot = (flat_ids[:, None] == jnp.arange(experts, dtype=jnp.int32)[None, :]).astype(jnp.int32)
    slot_rank = jnp.sum((jnp.cumsum(onehot, axis=0) - 1) * onehot, axis=1)
    scaled = (
        (gate_values[:, :, None] * cotangent[:, None, :].astype(jnp.float32))
        .astype(jnp.bfloat16)
        .reshape(assigns, feature_count)
    )
    zero_value = jnp.zeros((), jnp.bfloat16)
    send_mask = flat_ids >= 0
    bucket_rows = experts * capacity
    slot_index = flat_ids * capacity + slot_rank
    target = jnp.where(send_mask, slot_index, bucket_rows)
    slot_source = (
        jnp.full((bucket_rows,), assigns, jnp.int32).at[target].set(positions, mode="drop")
    )
    filled = slot_source < assigns
    safe = jnp.minimum(slot_source, assigns - 1)
    sent_rows = jnp.where(filled[:, None], tokens[safe // top_count], zero_value).reshape(
        experts, capacity, feature_count
    )
    sent_scaled = jnp.where(filled[:, None], scaled[safe], zero_value).reshape(
        experts, capacity, feature_count
    )
    recv_rows, recv_scaled = (
        lax.all_to_all(sent_rows, "expert", split_axis=0, concat_axis=0, tiled=True),
        lax.all_to_all(sent_scaled, "expert", split_axis=0, concat_axis=0, tiled=True),
    )
    hidden_act, expert_out = expert_apply(
        recv_rows.reshape(bucket_rows, feature_count), gate_up[0], down[0], hidden_count
    )
    gradient = outer_sum(hidden_act, recv_scaled.reshape(bucket_rows, feature_count))
    returned_rows = lax.all_to_all(
        expert_out.reshape(experts, capacity, feature_count),
        "expert",
        split_axis=0,
        concat_axis=0,
        tiled=True,
    )
    returned_rows = returned_rows.reshape(bucket_rows, feature_count)
    picked = returned_rows[jnp.where(send_mask, slot_index, 0)]
    weighted = gate_values[:, :, None] * picked.reshape(tok_rows, top_count, feature_count).astype(
        jnp.float32
    )
    mixed = jnp.sum(weighted, axis=1).astype(jnp.bfloat16)
    gradient = lax.psum(gradient, "dp")
    new_down, new_first, new_second = adamw(gradient, down[0], moment_first[0], moment_second[0])
    return (mixed, new_down[None], new_first[None], new_second[None])


MESH = pl.DeviceIdType.MESH
CHUNKS = 4
PIECES = 2
SIDE = 4
EXPERTS = 8


def fused_kernel(
    weights_ref, tokens_ref, cot_ref, gate_up_hbm, down_hbm, mixed_ref, grad_ref, gate_up, down,
    toks, cots, w_recv, w_cols, hidden, hidden_t, scaled, parts, peer_parts, from_left,
    from_right, acc, grad, grad_send, grad_recv, grad_all, acc_grad,
    load_sem, w_send, w_recv_sem, tok_send, tok_recv, cot_send, cot_recv,
    part_send, part_recv, sum_send, left_recv, right_recv, gs_send, gs_recv, ga_send, ga_recv,
):
    expert = lax.axis_index("expert")
    group = lax.axis_index("dp")
    chip = expert // 2
    core = expert % 2
    other = 1 - core
    rows, width = tokens_ref.shape
    half = down.shape[0]
    cw = width // CHUNKS
    quarter = half // 4
    group_x, group_y = group % 2, group // 2
    peer = chip * 2 + other
    right = jnp.minimum(chip + 1, SIDE - 1) * 2 + core
    left = jnp.maximum(chip - 1, 0) * 2 + core

    def dp_peer(k):
        px = group_x if k == 2 else 1 - group_x
        py = group_y if k == 1 else 1 - group_y
        return py * 2 + px

    def order(j):
        near = chip + 1 - 2 * (chip % 2)
        low = chip < 2
        return (chip, near, jnp.where(low, 2, 1), jnp.where(low, 3, 0))[j]

    def remote(src, dst, send, recv, target, axis="expert"):
        return pltpu.make_async_remote_copy(
            src_ref=src, dst_ref=dst, send_sem=send, recv_sem=recv,
            device_id={axis: target}, device_id_type=MESH,
        )

    loads = [
        pltpu.make_async_copy(src, dst, load_sem.at[i])
        for i, (src, dst) in enumerate(
            (
                (gate_up_hbm.at[0], gate_up),
                (down_hbm.at[0], down),
            )
        )
    ]
    for load in loads:
        load.start()

    barrier = pltpu.get_barrier_semaphore()
    for k in range(1, EXPERTS):
        pl.semaphore_signal(
            barrier, inc=1, device_id={"expert": (expert + k) % EXPERTS}, device_id_type=MESH
        )
    for k in range(1, 4):
        pl.semaphore_signal(barrier, inc=1, device_id={"dp": dp_peer(k)}, device_id_type=MESH)
    toks[chip, core] = tokens_ref[...]
    for n in range(CHUNKS):
        cots[n, chip, core] = cot_ref[:, n * cw : (n + 1) * cw]
    w_recv[expert] = weights_ref[expert]
    pl.semaphore_wait(barrier, EXPERTS + 2)

    def w_copy(k):
        target = (expert + k) % EXPERTS
        return remote(
            weights_ref.at[target], w_recv.at[expert], w_send.at[k - 1], w_recv_sem.at[k - 1], target
        )

    def w_arrival(k):
        source = (expert + EXPERTS - k) % EXPERTS
        return remote(
            weights_ref.at[source], w_recv.at[source], w_send.at[k - 1], w_recv_sem.at[k - 1], source
        )

    def gather_copies(view, send, recv, j):
        b = order(j)
        block = view(b, core)
        return (
            remote(block, block, send.at[j, 0], recv.at[b, core], right),
            remote(block, block, send.at[j, 1], recv.at[b, core], left),
            remote(block, block, send.at[j, 2], recv.at[b, core], peer),
        )

    def forward(view, send, recv, j):
        b = order(j)
        to_right, to_left, to_peer = gather_copies(view, send, recv, j)
        if j > 0:
            to_right.wait_recv()

        @pl.when((b <= chip) & (chip < SIDE - 1))
        def _():
            to_right.start()

        @pl.when((b >= chip) & (chip > 0))
        def _():
            to_left.start()

        to_peer.start()

    def from_peer(view, send, recv, j):
        b = order(j)
        block = view(b, other)
        remote(block, block, send.at[j, 2], recv.at[b, other], peer).wait_recv()

    def drain(view, send, recv, j):
        b = order(j)
        to_right, to_left, to_peer = gather_copies(view, send, recv, j)

        @pl.when((b <= chip) & (chip < SIDE - 1))
        def _():
            to_right.wait_send()

        @pl.when((b >= chip) & (chip > 0))
        def _():
            to_left.wait_send()

        to_peer.wait_send()

    piece = rows // PIECES

    def tok_args(h):
        return (
            lambda b, c: toks.at[b, c, pl.ds(h * piece, piece)], tok_send.at[h], tok_recv.at[h]
        )

    def cot_args(n):
        return (lambda b, c: cots.at[n, b, c], cot_send.at[n], cot_recv.at[n])

    def part_copy(b):
        return remote(
            parts.at[b, other], peer_parts.at[b], part_send.at[b], part_recv.at[b], peer
        )

    def run_expert(j):
        b = order(j)
        tile = 256

        @pl.loop(0, half // tile)
        def _(n):
            x = toks[b].reshape(2 * rows, width)
            lo = pl.multiple_of(n * tile, tile)
            hi = pl.multiple_of(half + n * tile, tile)
            gate = jnp.dot(x, gate_up[:, pl.ds(lo, tile)], preferred_element_type=jnp.float32)
            up = jnp.dot(x, gate_up[:, pl.ds(hi, tile)], preferred_element_type=jnp.float32)
            act = gate / (1.0 + jnp.exp(-gate)) * up
            hidden[:, pl.ds(lo, tile)] = act.astype(jnp.bfloat16)
            at = pl.multiple_of(b * 2 * rows, 2 * rows)
            hidden_t[pl.ds(lo, tile), pl.ds(at, 2 * rows)] = act.T.astype(jnp.bfloat16)

        @pl.loop(0, width // 512)
        def _(n):
            at = pl.multiple_of(n * 512, 512)
            out = jnp.dot(
                hidden[...], down[:, pl.ds(at, 512)], preferred_element_type=jnp.float32
            )
            w = w_cols[b].reshape(2 * rows, 128)[:, 0:1]
            parts[b, :, :, pl.ds(at, 512)] = (w * out).astype(jnp.bfloat16).reshape(2, rows, 512)

        part_copy(b).start()

    def sum_copies(b):
        block = parts.at[b, core]
        return (
            remote(block, from_left.at[b], sum_send.at[b], left_recv.at[b], right),
            remote(block, from_right.at[b], sum_send.at[b], right_recv.at[b], left),
        )

    def reduce_step(j):
        b = order(j)
        to_right, to_left = sum_copies(b)
        part_copy(b).wait_recv()
        acc[...] = parts[b, core].astype(jnp.float32) + peer_parts[b].astype(jnp.float32)

        @pl.when((b >= chip) & (chip > 0))
        def _():
            to_right.wait_recv()
            acc[...] += from_left[b].astype(jnp.float32)

        @pl.when((b <= chip) & (chip < SIDE - 1))
        def _():
            to_left.wait_recv()
            acc[...] += from_right[b].astype(jnp.float32)

        if j == 0:
            mixed_ref[...] = acc[...].astype(jnp.bfloat16)
        else:
            parts[b, core] = acc[...].astype(jnp.bfloat16)

            @pl.when(b > chip)
            def _():
                to_right.start()

            @pl.when(b < chip)
            def _():
                to_left.start()

    def scatter_copy(n, k):
        return remote(
            grad_send.at[n, dp_peer(k)], grad_recv.at[n, k - 1], gs_send.at[n, k - 1],
            gs_recv.at[n, k - 1], dp_peer(k), "dp",
        )

    def spread_copy(n, k, owner):
        block = grad_all.at[n, owner]
        return remote(
            block, block, ga_send.at[n, k - 1], ga_recv.at[n, k - 1], dp_peer(k), "dp"
        )

    def gradient(n):
        @pl.loop(0, SIDE)
        def _(b):
            w = w_cols[b].reshape(2 * rows, 128)[:, 0:1]
            cot = cots[n, b].reshape(2 * rows, cw).astype(jnp.float32)
            scaled[pl.ds(pl.multiple_of(b * 2 * rows, 2 * rows), 2 * rows), :] = (w * cot).astype(
                jnp.bfloat16
            )

        @pl.loop(0, 2)
        def _(m):
            at = pl.multiple_of(m * 2 * quarter, 2 * quarter)
            g = jnp.dot(
                hidden_t[pl.ds(at, 2 * quarter), :], scaled[...], preferred_element_type=jnp.float32
            )
            g = g.reshape(2, quarter, cw)
            grad[pl.ds(m * 2, 2)] = g
            grad_send[n, pl.ds(m * 2, 2)] = g.astype(jnp.bfloat16)

        for k in range(1, 4):
            scatter_copy(n, k).start()
        acc_grad[n] = grad[group]

    def spread(n):
        total = acc_grad[n]
        for k in range(1, 4):
            scatter_copy(n, k).wait_recv()
            total = total + grad_recv[n, k - 1].astype(jnp.float32)
        grad_all[n, group] = total.astype(jnp.bfloat16)
        for k in range(1, 4):
            spread_copy(n, k, group).start()

    def collect(n):
        for k in range(1, 4):
            spread_copy(n, k, dp_peer(k)).wait_recv()
        for q in range(4):
            grad_ref[q * quarter : (q + 1) * quarter, n * cw : (n + 1) * cw] = grad_all[n, q]

    is_end = (chip == 0) | (chip == SIDE - 1)

    def end_reduce(j):
        pl.when(is_end)(lambda: reduce_step(j))

    def middle_reduce(j):
        pl.when(jnp.logical_not(is_end))(lambda: reduce_step(j))

    for k in range(1, EXPERTS):
        w_copy(k).start()
    for h in range(PIECES):
        forward(*tok_args(h), 0)
    for k in range(1, EXPERTS):
        w_arrival(k).wait_recv()
    for s in range(EXPERTS):
        w_cols[s // 2, s % 2] = jnp.broadcast_to(w_recv[s][0:1, :], (128, 128)).T
    for load in loads:
        load.wait()
    def pass_on(j):
        for h in range(PIECES):
            forward(*tok_args(h), j)

    is_middle = jnp.logical_not(is_end)
    for j in range(SIDE):
        if j == 1:
            pass_on(1)
        if j >= 2:
            pl.when(is_end)(lambda: pass_on(j))
        if 1 <= j < SIDE - 1:
            pl.when(is_middle)(lambda: pass_on(j + 1))
        if j == 2:
            forward(*cot_args(0), 0)
            forward(*cot_args(1), 0)
        if j >= 2:
            end_reduce(j - 1)
        for h in range(PIECES):
            from_peer(*tok_args(h), j)
        run_expert(j)
    forward(*cot_args(0), 1)
    forward(*cot_args(0), 2)
    end_reduce(SIDE - 1)
    for n in range(CHUNKS):
        if n + 2 < CHUNKS:
            forward(*cot_args(n + 2), 0)
        forward(*cot_args(n), 3)
        if n + 1 < CHUNKS:
            forward(*cot_args(n + 1), 1)
            forward(*cot_args(n + 1), 2)
        if n >= 1:
            middle_reduce((2, 3, 1)[n - 1])
        for j in range(SIDE):
            from_peer(*cot_args(n), j)
        gradient(n)
        if n >= 1:
            spread(n - 1)
        if n >= 2:
            collect(n - 2)
    reduce_step(0)
    spread(CHUNKS - 1)
    collect(CHUNKS - 2)
    collect(CHUNKS - 1)
    for j in range(SIDE):
        for h in range(PIECES):
            drain(*tok_args(h), j)
        for n in range(CHUNKS):
            drain(*cot_args(n), j)
        part_copy(order(j)).wait_send()
        if j > 0:
            sum_copies(order(j))[0].wait_send()
    for k in range(1, EXPERTS):
        w_copy(k).wait_send()
    for n in range(CHUNKS):
        for k in range(1, 4):
            scatter_copy(n, k).wait_send()
            spread_copy(n, k, group).wait_send()


def fused_body(tokens, expert_ids, gate_values, gate_up, down, first, second, cotangent):
    rows, width = tokens.shape
    half = down.shape[1]
    cw = width // CHUNKS
    quarter = half // 4
    chosen = expert_ids[None] == jnp.arange(EXPERTS, dtype=jnp.int32)[:, None, None]
    weights = jnp.sum(jnp.where(chosen, gate_values[None], 0.0), axis=2)
    weights = jnp.broadcast_to(weights[:, None, :], (EXPERTS, 8, rows))
    bf, f32 = jnp.bfloat16, jnp.float32
    vmem = pl.BlockSpec(memory_space=pltpu.VMEM)
    hbm = pl.BlockSpec(memory_space=pl.ANY)
    dma = pltpu.SemaphoreType.DMA
    buffers = [
        ((width, 2 * half), bf), ((half, width), bf),
        ((SIDE, 2, rows, width), bf), ((CHUNKS, SIDE, 2, rows, cw), bf),
        ((EXPERTS, 8, rows), f32), ((SIDE, 2, rows, 128), f32),
        ((2 * rows, half), bf), ((half, EXPERTS * rows), bf), ((EXPERTS * rows, cw), bf),
        ((SIDE, 2, rows, width), bf), ((SIDE, rows, width), bf), ((SIDE, rows, width), bf),
        ((SIDE, rows, width), bf), ((rows, width), f32), ((4, quarter, cw), f32),
        ((CHUNKS, 4, quarter, cw), bf), ((CHUNKS, 3, quarter, cw), bf),
        ((CHUNKS, 4, quarter, cw), bf), ((CHUNKS, quarter, cw), f32),
    ]
    semaphores = [
        (2,), (EXPERTS - 1,), (EXPERTS - 1,), (PIECES, SIDE, 3), (PIECES, SIDE, 2), (CHUNKS, SIDE, 3),
        (CHUNKS, SIDE, 2), (SIDE,), (SIDE,), (SIDE,), (SIDE,), (SIDE,), (CHUNKS, 3), (CHUNKS, 3),
        (CHUNKS, 3), (CHUNKS, 3),
    ]
    mixed, gradient = pl.pallas_call(
        fused_kernel,
        out_shape=(
            jax.ShapeDtypeStruct((rows, width), bf), jax.ShapeDtypeStruct((half, width), bf)
        ),
        in_specs=[vmem, vmem, vmem, hbm, hbm],
        out_specs=(vmem, vmem),
        scratch_shapes=[pltpu.VMEM(s, t) for s, t in buffers] + [dma(s) for s in semaphores],
        compiler_params=pltpu.CompilerParams(
            collective_id=0, has_side_effects=True, vmem_limit_bytes=56 * 1024 * 1024
        ),
    )(weights, tokens, cotangent, gate_up, down)
    states = adamw(gradient[None].astype(f32), down, first, second)
    return (mixed, *states)


def solution(mesh):
    def choose(*args):
        fits = mesh.shape["expert"] == 8 and mesh.shape["dp"] == 4 and args[0].shape[0] == 128
        return (fused_body if fits else body)(*args)

    return jax.shard_map(
        choose,
        mesh=mesh,
        in_specs=(
            P(("dp", "expert"), None),
            P(("dp", "expert"), None),
            P(("dp", "expert"), None),
            P("expert", None, None),
            P("expert", None, None),
            P("expert", None, None),
            P("expert", None, None),
            P(("dp", "expert"), None),
        ),
        out_specs=(
            P(("dp", "expert"), None),
            P("expert", None, None),
            P("expert", None, None),
            P("expert", None, None),
        ),
        check_vma=False,
    )
```

```python
import jax
import jax.numpy as jnp
from jax import lax
from jax.experimental import pallas as pl
from jax.experimental.pallas import tpu as pltpu
from jax.sharding import PartitionSpec as P

beta_one = 0.9
beta_two = 0.95
learn_rate = 0.01
decay_rate = 0.1
eps_value = 1e-08
first_fix = 1.0 - 0.9**10
second_fix = 1.0 - 0.95**10


def expert_apply(rows, gate_up_w, down_w, feature_half):
    projected = jnp.dot(rows, gate_up_w, preferred_element_type=jnp.float32)
    hidden_act = (jax.nn.silu(projected[:, :feature_half]) * projected[:, feature_half:]).astype(
        jnp.bfloat16
    )
    expert_out = jnp.dot(hidden_act, down_w, preferred_element_type=jnp.float32).astype(
        jnp.bfloat16
    )
    return (hidden_act, expert_out)


def adamw(gradient, down_w, first_old, second_old):
    first_new = beta_one * first_old.astype(jnp.float32) + (1.0 - beta_one) * gradient
    second_new = beta_two * second_old.astype(jnp.float32) + (1.0 - beta_two) * gradient * gradient
    second_hat = second_new * (1.0 / second_fix)
    step_size = first_new * (learn_rate / first_fix) / (second_hat * lax.rsqrt(second_hat) + eps_value)
    down_new = down_w.astype(jnp.float32) * (1.0 - learn_rate * decay_rate) - step_size
    return (
        down_new.astype(jnp.bfloat16),
        first_new.astype(jnp.bfloat16),
        second_new.astype(jnp.bfloat16),
    )


def outer_sum(hidden_act, scaled_rows):
    return lax.dot_general(
        hidden_act, scaled_rows, (((0,), (0,)), ((), ())), preferred_element_type=jnp.float32
    )


def body(tokens, expert_ids, gate_values, gate_up, down, moment_first, moment_second, cotangent):
    tok_rows, feature_count = tokens.shape
    top_count = expert_ids.shape[1]
    hidden_count = down.shape[1]
    experts = lax.axis_size("expert")
    capacity = tok_rows // 2
    flat_ids = expert_ids.reshape(-1)
    assigns = flat_ids.shape[0]
    positions = jnp.arange(assigns, dtype=jnp.int32)
    onehot = (flat_ids[:, None] == jnp.arange(experts, dtype=jnp.int32)[None, :]).astype(jnp.int32)
    slot_rank = jnp.sum((jnp.cumsum(onehot, axis=0) - 1) * onehot, axis=1)
    scaled = (
        (gate_values[:, :, None] * cotangent[:, None, :].astype(jnp.float32))
        .astype(jnp.bfloat16)
        .reshape(assigns, feature_count)
    )
    zero_value = jnp.zeros((), jnp.bfloat16)
    send_mask = flat_ids >= 0
    bucket_rows = experts * capacity
    slot_index = flat_ids * capacity + slot_rank
    target = jnp.where(send_mask, slot_index, bucket_rows)
    slot_source = (
        jnp.full((bucket_rows,), assigns, jnp.int32).at[target].set(positions, mode="drop")
    )
    filled = slot_source < assigns
    safe = jnp.minimum(slot_source, assigns - 1)
    sent_rows = jnp.where(filled[:, None], tokens[safe // top_count], zero_value).reshape(
        experts, capacity, feature_count
    )
    sent_scaled = jnp.where(filled[:, None], scaled[safe], zero_value).reshape(
        experts, capacity, feature_count
    )
    recv_rows, recv_scaled = (
        lax.all_to_all(sent_rows, "expert", split_axis=0, concat_axis=0, tiled=True),
        lax.all_to_all(sent_scaled, "expert", split_axis=0, concat_axis=0, tiled=True),
    )
    hidden_act, expert_out = expert_apply(
        recv_rows.reshape(bucket_rows, feature_count), gate_up[0], down[0], hidden_count
    )
    gradient = outer_sum(hidden_act, recv_scaled.reshape(bucket_rows, feature_count))
    returned_rows = lax.all_to_all(
        expert_out.reshape(experts, capacity, feature_count),
        "expert",
        split_axis=0,
        concat_axis=0,
        tiled=True,
    )
    returned_rows = returned_rows.reshape(bucket_rows, feature_count)
    picked = returned_rows[jnp.where(send_mask, slot_index, 0)]
    weighted = gate_values[:, :, None] * picked.reshape(tok_rows, top_count, feature_count).astype(
        jnp.float32
    )
    mixed = jnp.sum(weighted, axis=1).astype(jnp.bfloat16)
    gradient = lax.psum(gradient, "dp")
    new_down, new_first, new_second = adamw(gradient, down[0], moment_first[0], moment_second[0])
    return (mixed, new_down[None], new_first[None], new_second[None])


MESH = pl.DeviceIdType.MESH
CHUNKS = 4
PIECES = 2
SIDE = 4
EXPERTS = 8


def fused_kernel(
    weights_ref, tokens_ref, cot_ref, gate_up_hbm, down_hbm, mixed_ref, grad_ref, gate_up, down,
    toks, cots, w_recv, w_cols, hidden, hidden_t, scaled, parts, peer_parts, from_left,
    from_right, acc, grad, grad_send, grad_recv, grad_all, acc_grad,
    load_sem, w_send, w_recv_sem, tok_send, tok_recv, cot_send, cot_recv,
    part_send, part_recv, sum_send, left_recv, right_recv, gs_send, gs_recv, ga_send, ga_recv,
):
    expert = lax.axis_index("expert")
    group = lax.axis_index("dp")
    chip = expert // 2
    core = expert % 2
    other = 1 - core
    rows, width = tokens_ref.shape
    half = down.shape[0]
    cw = width // CHUNKS
    quarter = half // 4
    group_x, group_y = group % 2, group // 2
    peer = chip * 2 + other
    right = jnp.minimum(chip + 1, SIDE - 1) * 2 + core
    left = jnp.maximum(chip - 1, 0) * 2 + core

    def dp_peer(k):
        px = group_x if k == 2 else 1 - group_x
        py = group_y if k == 1 else 1 - group_y
        return py * 2 + px

    def order(j):
        near = chip + 1 - 2 * (chip % 2)
        low = chip < 2
        return (chip, near, jnp.where(low, 2, 1), jnp.where(low, 3, 0))[j]

    def remote(src, dst, send, recv, target, axis="expert"):
        return pltpu.make_async_remote_copy(
            src_ref=src, dst_ref=dst, send_sem=send, recv_sem=recv,
            device_id={axis: target}, device_id_type=MESH,
        )

    loads = [
        pltpu.make_async_copy(src, dst, load_sem.at[i])
        for i, (src, dst) in enumerate(
            (
                (gate_up_hbm.at[0], gate_up),
                (down_hbm.at[0], down),
            )
        )
    ]
    for load in loads:
        load.start()

    barrier = pltpu.get_barrier_semaphore()
    for k in range(1, EXPERTS):
        pl.semaphore_signal(
            barrier, inc=1, device_id={"expert": (expert + k) % EXPERTS}, device_id_type=MESH
        )
    for k in range(1, 4):
        pl.semaphore_signal(barrier, inc=1, device_id={"dp": dp_peer(k)}, device_id_type=MESH)
    toks[chip, core] = tokens_ref[...]
    for n in range(CHUNKS):
        cots[n, chip, core] = cot_ref[:, n * cw : (n + 1) * cw]
    w_recv[expert] = weights_ref[expert]
    pl.semaphore_wait(barrier, EXPERTS + 2)

    def w_copy(k):
        target = (expert + k) % EXPERTS
        return remote(
            weights_ref.at[target], w_recv.at[expert], w_send.at[k - 1], w_recv_sem.at[k - 1], target
        )

    def w_arrival(k):
        source = (expert + EXPERTS - k) % EXPERTS
        return remote(
            weights_ref.at[source], w_recv.at[source], w_send.at[k - 1], w_recv_sem.at[k - 1], source
        )

    def gather_copies(view, send, recv, j):
        b = order(j)
        block = view(b, core)
        return (
            remote(block, block, send.at[j, 0], recv.at[b, core], right),
            remote(block, block, send.at[j, 1], recv.at[b, core], left),
            remote(block, block, send.at[j, 2], recv.at[b, core], peer),
        )

    def forward(view, send, recv, j):
        b = order(j)
        to_right, to_left, to_peer = gather_copies(view, send, recv, j)
        if j > 0:
            to_right.wait_recv()

        @pl.when((b <= chip) & (chip < SIDE - 1))
        def _():
            to_right.start()

        @pl.when((b >= chip) & (chip > 0))
        def _():
            to_left.start()

        to_peer.start()

    def from_peer(view, send, recv, j):
        b = order(j)
        block = view(b, other)
        remote(block, block, send.at[j, 2], recv.at[b, other], peer).wait_recv()

    def drain(view, send, recv, j):
        b = order(j)
        to_right, to_left, to_peer = gather_copies(view, send, recv, j)

        @pl.when((b <= chip) & (chip < SIDE - 1))
        def _():
            to_right.wait_send()

        @pl.when((b >= chip) & (chip > 0))
        def _():
            to_left.wait_send()

        to_peer.wait_send()

    piece = rows // PIECES

    def tok_args(h):
        return (
            lambda b, c: toks.at[b, c, pl.ds(h * piece, piece)], tok_send.at[h], tok_recv.at[h]
        )

    def cot_args(n):
        return (lambda b, c: cots.at[n, b, c], cot_send.at[n], cot_recv.at[n])

    def part_copy(b):
        return remote(
            parts.at[b, other], peer_parts.at[b], part_send.at[b], part_recv.at[b], peer
        )

    def run_expert(j):
        b = order(j)
        tile = 256

        @pl.loop(0, half // tile)
        def _(n):
            x = toks[b].reshape(2 * rows, width)
            lo = pl.multiple_of(n * tile, tile)
            hi = pl.multiple_of(half + n * tile, tile)
            gate = jnp.dot(x, gate_up[:, pl.ds(lo, tile)], preferred_element_type=jnp.float32)
            up = jnp.dot(x, gate_up[:, pl.ds(hi, tile)], preferred_element_type=jnp.float32)
            act = gate / (1.0 + jnp.exp(-gate)) * up
            hidden[:, pl.ds(lo, tile)] = act.astype(jnp.bfloat16)
            at = pl.multiple_of(b * 2 * rows, 2 * rows)
            hidden_t[pl.ds(lo, tile), pl.ds(at, 2 * rows)] = act.T.astype(jnp.bfloat16)

        @pl.loop(0, width // 512)
        def _(n):
            at = pl.multiple_of(n * 512, 512)
            out = jnp.dot(
                hidden[...], down[:, pl.ds(at, 512)], preferred_element_type=jnp.float32
            )
            w = w_cols[b].reshape(2 * rows, 128)[:, 0:1]
            parts[b, :, :, pl.ds(at, 512)] = (w * out).astype(jnp.bfloat16).reshape(2, rows, 512)

        part_copy(b).start()

    def sum_copies(b):
        block = parts.at[b, core]
        return (
            remote(block, from_left.at[b], sum_send.at[b], left_recv.at[b], right),
            remote(block, from_right.at[b], sum_send.at[b], right_recv.at[b], left),
        )

    def reduce_step(j):
        b = order(j)
        to_right, to_left = sum_copies(b)
        part_copy(b).wait_recv()
        acc[...] = parts[b, core].astype(jnp.float32) + peer_parts[b].astype(jnp.float32)

        @pl.when((b >= chip) & (chip > 0))
        def _():
            to_right.wait_recv()
            acc[...] += from_left[b].astype(jnp.float32)

        @pl.when((b <= chip) & (chip < SIDE - 1))
        def _():
            to_left.wait_recv()
            acc[...] += from_right[b].astype(jnp.float32)

        if j == 0:
            mixed_ref[...] = acc[...].astype(jnp.bfloat16)
        else:
            parts[b, core] = acc[...].astype(jnp.bfloat16)

            @pl.when(b > chip)
            def _():
                to_right.start()

            @pl.when(b < chip)
            def _():
                to_left.start()

    def scatter_copy(n, k):
        return remote(
            grad_send.at[n, dp_peer(k)], grad_recv.at[n, k - 1], gs_send.at[n, k - 1],
            gs_recv.at[n, k - 1], dp_peer(k), "dp",
        )

    def spread_copy(n, k, owner):
        block = grad_all.at[n, owner]
        return remote(
            block, block, ga_send.at[n, k - 1], ga_recv.at[n, k - 1], dp_peer(k), "dp"
        )

    def gradient(n):
        @pl.loop(0, SIDE)
        def _(b):
            w = w_cols[b].reshape(2 * rows, 128)[:, 0:1]
            cot = cots[n, b].reshape(2 * rows, cw).astype(jnp.float32)
            scaled[pl.ds(pl.multiple_of(b * 2 * rows, 2 * rows), 2 * rows), :] = (w * cot).astype(
                jnp.bfloat16
            )

        @pl.loop(0, 2)
        def _(m):
            at = pl.multiple_of(m * 2 * quarter, 2 * quarter)
            g = jnp.dot(
                hidden_t[pl.ds(at, 2 * quarter), :], scaled[...], preferred_element_type=jnp.float32
            )
            g = g.reshape(2, quarter, cw)
            grad[pl.ds(m * 2, 2)] = g
            grad_send[n, pl.ds(m * 2, 2)] = g.astype(jnp.bfloat16)

        for k in range(1, 4):
            scatter_copy(n, k).start()
        acc_grad[n] = grad[group]

    def spread(n):
        total = acc_grad[n]
        for k in range(1, 4):
            scatter_copy(n, k).wait_recv()
            total = total + grad_recv[n, k - 1].astype(jnp.float32)
        grad_all[n, group] = total.astype(jnp.bfloat16)
        for k in range(1, 4):
            spread_copy(n, k, group).start()

    def collect(n):
        for k in range(1, 4):
            spread_copy(n, k, dp_peer(k)).wait_recv()
        for q in range(4):
            grad_ref[q * quarter : (q + 1) * quarter, n * cw : (n + 1) * cw] = grad_all[n, q]

    is_end = (chip == 0) | (chip == SIDE - 1)

    def end_reduce(j):
        pl.when(is_end)(lambda: reduce_step(j))

    def middle_reduce(j):
        pl.when(jnp.logical_not(is_end))(lambda: reduce_step(j))

    for k in range(1, EXPERTS):
        w_copy(k).start()
    for h in range(PIECES):
        forward(*tok_args(h), 0)
    for k in range(1, EXPERTS):
        w_arrival(k).wait_recv()
    for s in range(EXPERTS):
        w_cols[s // 2, s % 2] = jnp.broadcast_to(w_recv[s][0:1, :], (128, 128)).T
    for load in loads:
        load.wait()
    def pass_on(j):
        for h in range(PIECES):
            forward(*tok_args(h), j)

    is_middle = jnp.logical_not(is_end)
    for j in range(SIDE):
        if j == 1:
            pass_on(1)
        if j >= 2:
            pl.when(is_end)(lambda: pass_on(j))
        if 1 <= j < SIDE - 1:
            pl.when(is_middle)(lambda: pass_on(j + 1))
        if j == 2:
            forward(*cot_args(0), 0)
            forward(*cot_args(1), 0)
            forward(*cot_args(2), 0)
        if j >= 2:
            end_reduce(j - 1)
        for h in range(PIECES):
            from_peer(*tok_args(h), j)
        run_expert(j)
    forward(*cot_args(0), 1)
    forward(*cot_args(0), 2)
    end_reduce(SIDE - 1)
    for n in range(CHUNKS):
        if n + 3 < CHUNKS:
            forward(*cot_args(n + 3), 0)
        forward(*cot_args(n), 3)
        if n + 1 < CHUNKS:
            forward(*cot_args(n + 1), 1)
            forward(*cot_args(n + 1), 2)
        if n >= 1:
            middle_reduce((2, 3, 1)[n - 1])
        for j in range(SIDE):
            from_peer(*cot_args(n), j)
        gradient(n)
        if n >= 1:
            spread(n - 1)
        if n >= 2:
            collect(n - 2)
    reduce_step(0)
    spread(CHUNKS - 1)
    collect(CHUNKS - 2)
    collect(CHUNKS - 1)
    for j in range(SIDE):
        for h in range(PIECES):
            drain(*tok_args(h), j)
        for n in range(CHUNKS):
            drain(*cot_args(n), j)
        part_copy(order(j)).wait_send()
        if j > 0:
            sum_copies(order(j))[0].wait_send()
    for k in range(1, EXPERTS):
        w_copy(k).wait_send()
    for n in range(CHUNKS):
        for k in range(1, 4):
            scatter_copy(n, k).wait_send()
            spread_copy(n, k, group).wait_send()


def fused_body(tokens, expert_ids, gate_values, gate_up, down, first, second, cotangent):
    rows, width = tokens.shape
    half = down.shape[1]
    cw = width // CHUNKS
    quarter = half // 4
    chosen = expert_ids[None] == jnp.arange(EXPERTS, dtype=jnp.int32)[:, None, None]
    weights = jnp.sum(jnp.where(chosen, gate_values[None], 0.0), axis=2)
    weights = jnp.broadcast_to(weights[:, None, :], (EXPERTS, 8, rows))
    bf, f32 = jnp.bfloat16, jnp.float32
    vmem = pl.BlockSpec(memory_space=pltpu.VMEM)
    hbm = pl.BlockSpec(memory_space=pl.ANY)
    dma = pltpu.SemaphoreType.DMA
    buffers = [
        ((width, 2 * half), bf), ((half, width), bf),
        ((SIDE, 2, rows, width), bf), ((CHUNKS, SIDE, 2, rows, cw), bf),
        ((EXPERTS, 8, rows), f32), ((SIDE, 2, rows, 128), f32),
        ((2 * rows, half), bf), ((half, EXPERTS * rows), bf), ((EXPERTS * rows, cw), bf),
        ((SIDE, 2, rows, width), bf), ((SIDE, rows, width), bf), ((SIDE, rows, width), bf),
        ((SIDE, rows, width), bf), ((rows, width), f32), ((4, quarter, cw), f32),
        ((CHUNKS, 4, quarter, cw), bf), ((CHUNKS, 3, quarter, cw), bf),
        ((CHUNKS, 4, quarter, cw), bf), ((CHUNKS, quarter, cw), f32),
    ]
    semaphores = [
        (2,), (EXPERTS - 1,), (EXPERTS - 1,), (PIECES, SIDE, 3), (PIECES, SIDE, 2), (CHUNKS, SIDE, 3),
        (CHUNKS, SIDE, 2), (SIDE,), (SIDE,), (SIDE,), (SIDE,), (SIDE,), (CHUNKS, 3), (CHUNKS, 3),
        (CHUNKS, 3), (CHUNKS, 3),
    ]
    mixed, gradient = pl.pallas_call(
        fused_kernel,
        out_shape=(
            jax.ShapeDtypeStruct((rows, width), bf), jax.ShapeDtypeStruct((half, width), bf)
        ),
        in_specs=[vmem, vmem, vmem, hbm, hbm],
        out_specs=(vmem, vmem),
        scratch_shapes=[pltpu.VMEM(s, t) for s, t in buffers] + [dma(s) for s in semaphores],
        compiler_params=pltpu.CompilerParams(
            collective_id=0, has_side_effects=True, vmem_limit_bytes=56 * 1024 * 1024
        ),
    )(weights, tokens, cotangent, gate_up, down)
    states = adamw(gradient[None].astype(f32), down, first, second)
    return (mixed, *states)


def solution(mesh):
    def choose(*args):
        fits = mesh.shape["expert"] == 8 and mesh.shape["dp"] == 4 and args[0].shape[0] == 128
        return (fused_body if fits else body)(*args)

    return jax.shard_map(
        choose,
        mesh=mesh,
        in_specs=(
            P(("dp", "expert"), None),
            P(("dp", "expert"), None),
            P(("dp", "expert"), None),
            P("expert", None, None),
            P("expert", None, None),
            P("expert", None, None),
            P("expert", None, None),
            P(("dp", "expert"), None),
        ),
        out_specs=(
            P(("dp", "expert"), None),
            P("expert", None, None),
            P("expert", None, None),
            P("expert", None, None),
        ),
        check_vma=False,
    )
```
